32 devices in a mesh: vocab: 8 (over z, y), token: 4 (over x, core).
Axes of the slice: x: 2, y: 2, z: 4, core: 2. Of those that a mesh axis runs over, the one named last changes fastest.
Arguments:
- hidden: bfloat16 [4096, 4096], P(('vocab', 'token')), may hold values from -16 to 16
- cand_embed: bfloat16 [1024, 4096], P('vocab'), may hold values from -0.5 to 0.5
- freq_embed: bfloat16 [32, 4096], P('vocab'), may hold values from -0.09375 to 0.09375
- owner_order: int32 [8], replicated, may hold values from 0 to 7, each once
- cand_blocks: int32 [512, 4], P(('vocab', 'token')), may hold values from 0 to 7, all different within a row; in each aligned block of 16 rows (0 to 15, 16 to 31, ...) at most 16 rows name the same one
- group_tokens: int32 [32, 128], P(('vocab', 'token')), may hold values from 0 to 127, each once within a row
- target_slot: int32 [4096], P(('vocab', 'token')), may hold values from 0 to 543
Outputs:
- logits: bfloat16 [4096, 544], P(('vocab', 'token'))
- loss: float32 [4096], P(('vocab', 'token'))
- grad_hidden: bfloat16 [4096, 4096], P(('vocab', 'token'))
- grad_cand: float32 [1024, 4096], P(('vocab', 'token'))
- grad_freq: float32 [32, 4096], P(('vocab', 'token'))
The draws below stay inside these ranges and needn't reach their ends.
Inputs may be any that keep to these rules, and one draw needn't show every extreme that they name: `cand_blocks`: each row names 4 different blocks. Among the 16 groups of one device no block is named by more than 16 groups, and some device reaches 16. `group_tokens`: each row lists every number below 128 once. `owner_order`: every number below 8 once.
All inputs are finite; a program needn't handle non-finite values.
Results may differ from the reference program's by a relative error of at most 0.0052.
Values may be sent and summed in bfloat16 or wider, within the bound.
A program may use at most 128 MiB of HBM per device.

```python
import math
import jax
import jax.numpy as jnp
import numpy as np
from jax import lax

D = 4096
BW = 128
K = 4
GTOK = 8
PANEL = 4
G_DEV = 16
TOK_DEV = 128
TOKENS = 4096
GROUPS = 512
CAP = 16
FREQ = 32
COLS = 544
POOL_WORDS = 1024
N_VOCAB = 8
DEVICES = 32


def draw_hidden(key, part):
    first, second = jax.random.split(key, 2)
    scales = jnp.exp(jax.random.uniform(second, (TOKENS, 1), jnp.float32, math.log(0.4), math.log(2.5)))
    values = jnp.clip(jax.random.normal(first, (TOKENS, D), jnp.float32), -6.0, 6.0) * scales
    return values.astype(jnp.bfloat16)


def draw_cand_embed(key, part):
    first, second = jax.random.split(key, 2)
    scales = jnp.exp(jax.random.uniform(second, (POOL_WORDS, 1), jnp.float32, math.log(0.4), math.log(2.5)))
    base = jnp.clip(jax.random.normal(first, (POOL_WORDS, D), jnp.float32), -6.0, 6.0)
    values = jnp.clip(base * scales * D ** (-0.5), -0.5, 0.5)
    return values.astype(jnp.bfloat16)


def plant(entries, key, smallest, largest):
    place = [jax.random.randint(jax.random.fold_in(key, axis), (), 0, length) for axis, length in enumerate(entries.shape)]
    main_axis = entries.shape.index(max(entries.shape))
    neighbour = place[:main_axis] + [(place[main_axis] + 1) % entries.shape[main_axis]] + place[main_axis + 1:]
    return entries.at[tuple(place)].set(smallest).at[tuple(neighbour)].set(largest)


def steps_of(own_key, shape, cuts, smallest, top_value):
    def one(dim, shards_of):
        heights = jax.random.uniform(jax.random.fold_in(jax.random.fold_in(own_key, 6), dim), (shards_of,), jnp.float32, smallest / len(cuts), top_value / len(cuts))
        return jnp.repeat(jnp.exp(heights), shape[dim] // shards_of).reshape((-1,) + (1,) * (len(shape) - dim - 1))

    level = one(*cuts[0])
    for cut in cuts[1:]:
        level = level * one(*cut)
    return level


def routed_block(own_key, own, number, rows, number_of, top, limit, skew):
    order = jax.random.permutation(own_key, number_of)
    packed, ordinary = load_shares(number_of, rows * top, limit, skew, True), load_shares(number_of, rows * top, limit, skew, False)
    places = jnp.arange(number_of)

    def named(tallies, rotation):
        used = int((tallies > 0).sum())
        fixed = max(1, used // 4)
        passed = fixed + (places - fixed + rotation * (used - fixed)) % max(1, number_of - fixed)
        return jnp.zeros((number_of,), jnp.int32).at[order[jnp.where(places < fixed, places, passed)]].set(jnp.asarray(tallies, jnp.int32))

    tallies = jnp.where(number % 4 == 0, named(packed, number // 4), named(ordinary, number - number // 4 - 1))
    mixed = jax.random.permutation(jax.random.fold_in(own, 3), number_of)
    giver, sink = mixed[0:number_of // 2 * 2:2], mixed[1:number_of // 2 * 2:2]
    margin = jnp.minimum(tallies[giver] - 1, limit - tallies[sink]) // 2
    margin = jnp.where((giver == order[0]) | (sink == order[0]) | (tallies[sink] == 0), 0, jnp.maximum(margin, 0))
    passed = jax.random.randint(jax.random.fold_in(own, 4), (number_of // 2,), 0, 1 << 20) % (margin + 1)
    tallies = tallies.at[giver].add(-passed).at[sink].add(passed)
    labels = jnp.searchsorted(jnp.cumsum(tallies), jnp.arange(rows * top), side="right").astype(jnp.int32)
    table = labels.reshape(top, rows).T
    table = table[jax.random.permutation(jax.random.fold_in(own, 1), rows)]
    rotation = jax.random.randint(jax.random.fold_in(own, 2), (rows, 1), 0, top)
    return jnp.take_along_axis(table, (jnp.arange(top)[None, :] + rotation) % top, axis=1)


def load_shares(number_of, total, most, slope, full):
    portions = [(1 << 20) // math.isqrt(grade ** slope) + 1 for grade in range(1, number_of + 1)]
    largest = most if full else min(most, max(-(-total // number_of), total * portions[0] // sum(portions)))
    least = 1 if total - largest >= number_of - 1 else 0
    counts, surplus = [largest] + [least] * (number_of - 1), total - largest - least * (number_of - 1)
    while surplus > 0:
        movable = [i for i in range(1, number_of) if counts[i] < largest] or [i for i in range(1, number_of) if counts[i] < most]
        pool, left = sum([portions[i] for i in movable]), surplus
        for i in movable:
            extra = min(most - counts[i], max(1, left * portions[i] // pool), surplus)
            counts[i] = counts[i] + extra
            surplus = surplus - extra
    return np.array(counts)


def noise(key, dims, scale, most, cuts=(), held_as=jnp.bfloat16):
    level = steps_of(key, dims, cuts, -0.22, 0.18) if cuts else 1.0
    drawn = jax.random.normal(key, dims, jnp.float32) * scale * level
    return jnp.minimum(jnp.maximum(drawn, -most), most).astype(held_as)


def setup_inputs(seed: int = 0) -> dict:
    splits = jax.random.split(jax.random.key(seed), 8)
    hidden = draw_hidden(jax.random.fold_in(splits[7], 71), 0)
    cand_embed = draw_cand_embed(jax.random.fold_in(splits[7], 71), 0)
    freq_embed = noise(splits[2], (FREQ, D), D ** -0.5, 0.09375, ((0, 8),))
    owner_order = jax.random.permutation(splits[3], N_VOCAB).astype(jnp.int32)
    cand_blocks_keys = jax.random.split(jax.random.fold_in(splits[4], 1), GROUPS // G_DEV)
    cand_blocks_turns = jax.random.permutation(jax.random.fold_in(splits[4], 3), GROUPS // G_DEV)
    cand_blocks = jax.vmap(lambda own, number: routed_block(jax.random.fold_in(splits[4], 2), own, number, G_DEV, N_VOCAB, K, CAP, 2))(cand_blocks_keys, cand_blocks_turns).reshape((GROUPS, K))
    group_tokens = jax.vmap(lambda own: jax.random.permutation(own, TOK_DEV))(jax.random.split(splits[5], DEVICES)).reshape((DEVICES, TOK_DEV)).astype(jnp.int32)
    target_slot = plant(jax.random.randint(splits[6], (TOKENS,), 0, COLS), jax.random.fold_in(splits[6], 1), 0, COLS - 1).astype(jnp.int32)
    return {"hidden": hidden, "cand_embed": cand_embed, "freq_embed": freq_embed, "owner_order": owner_order, "cand_blocks": cand_blocks, "group_tokens": group_tokens, "target_slot": target_slot}


def reference(hidden, cand_embed, freq_embed, owner_order, cand_blocks, group_tokens, target_slot):
    freq_table = freq_embed.reshape(N_VOCAB, PANEL, D)[owner_order].reshape(FREQ, D)
    freq_wide = freq_table.astype(jnp.float32)
    block_table = cand_embed.reshape(N_VOCAB, BW, D)
    columns = jnp.arange(COLS, dtype=jnp.int32)
    positions = jnp.arange(TOK_DEV, dtype=jnp.int32)

    def one_device(carry, inputs):
        cand_grad, freq_grad = carry
        device_rows, listing, device_targets, device_blocks = inputs
        gathered = device_rows[listing].reshape(G_DEV, GTOK, D).astype(jnp.float32)
        wanted = device_targets[listing].reshape(G_DEV, GTOK)
        chosen = block_table[device_blocks].astype(jnp.float32)
        freq_scores = jnp.einsum("gtd,fd->gtf", gathered, freq_wide)
        cand_scores = jnp.einsum("gtd,gkwd->gtkw", gathered, chosen).reshape(G_DEV, GTOK, K * BW)
        scores = jnp.concatenate([freq_scores, cand_scores], axis=-1)
        row_top = jnp.max(scores, axis=-1)
        exponentials = jnp.exp(scores - row_top[..., None])
        total = jnp.sum(exponentials, axis=-1)
        target_hot = (wanted[..., None] == columns).astype(jnp.float32)
        token_loss = jnp.log(total) + row_top - jnp.sum(target_hot * scores, axis=-1)
        prob_short = (exponentials * (1.0 / total)[..., None] - target_hot).astype(jnp.bfloat16)
        probgrad = lax.optimization_barrier(prob_short).astype(jnp.float32)
        prob_freq = probgrad[..., :FREQ]
        prob_cand = probgrad[..., FREQ:].reshape(G_DEV, GTOK, K, BW)
        part_short = jnp.einsum("gtkw,gkwd->gtkd", prob_cand, chosen).astype(jnp.bfloat16)
        block_part = lax.optimization_barrier(part_short).astype(jnp.float32)
        grad_rows = jnp.einsum("gtf,fd->gtd", prob_freq, freq_wide) + jnp.sum(block_part, axis=2)
        block_term = jnp.einsum("gtkw,gtd->gkwd", prob_cand, gathered).reshape(G_DEV * K, BW, D)
        cand_grad = cand_grad.at[device_blocks.reshape(G_DEV * K)].add(block_term)
        freq_grad = freq_grad + jnp.einsum("gtf,gtd->fd", prob_freq, gathered)
        undo = jnp.zeros((TOK_DEV,), jnp.int32).at[listing].set(positions)
        device_logits = scores.reshape(TOK_DEV, COLS).astype(jnp.bfloat16)[undo]
        device_loss = token_loss.reshape(TOK_DEV)[undo]
        device_grad = grad_rows.reshape(TOK_DEV, D).astype(jnp.bfloat16)[undo]
        return (cand_grad, freq_grad), (device_logits, device_loss, device_grad)

    start_carry = (jnp.zeros((N_VOCAB, BW, D), jnp.float32), jnp.zeros((FREQ, D), jnp.float32))
    inputs = (hidden.reshape(DEVICES, TOK_DEV, D), group_tokens,
              target_slot.reshape(DEVICES, TOK_DEV), cand_blocks.reshape(DEVICES, G_DEV, K))
    (cand_grad, freq_grad), (all_logits, all_loss, all_grad) = lax.scan(one_device, start_carry, inputs)
    grad_freq = jnp.zeros((N_VOCAB, PANEL, D), jnp.float32).at[owner_order].set(
        freq_grad.reshape(N_VOCAB, PANEL, D)).reshape(FREQ, D)
    return (all_logits.reshape(TOKENS, COLS), all_loss.reshape(TOKENS), all_grad.reshape(TOKENS, D),
            cand_grad.reshape(POOL_WORDS, D), grad_freq)
```

```python
import jax
import jax.numpy as jnp
from jax import lax
from jax.experimental import pallas as pl
from jax.experimental.pallas import tpu as pltpu
from jax.sharding import PartitionSpec as P

D = 4096
BW = 128
K = 4
GTOK = 8
PANEL = 4
G_DEV = 16


def token_blocks(cand_blocks, group_tokens):
    where = jnp.arange(group_tokens.shape[1], dtype=jnp.int32)
    held = group_tokens[0][None, :] == where[:, None]
    group = jnp.sum(jnp.where(held, (where // GTOK)[None, :], 0), axis=1)
    group_hot = group[:, None] == jnp.arange(cand_blocks.shape[0], dtype=jnp.int32)[None, :]
    return jnp.sum(jnp.where(group_hot[:, :, None], cand_blocks[None], 0), axis=1)


def ring(hidden, cand_embed, freq_embed, owner_order, cand_blocks, group_tokens, target_slot):
    owners, shards = lax.axis_size("vocab"), lax.axis_size("token")
    me, shard = lax.axis_index("vocab"), lax.axis_index("token")
    tokens = hidden.shape[0]
    freq_count = owners * PANEL
    blocks = token_blocks(cand_blocks, group_tokens)
    turn = [(i, (i + 1) % owners) for i in range(owners)]

    def pass_on(arrays):
        return tuple(lax.ppermute(a, "vocab", turn) for a in arrays)

    def forward(step, carry):
        cand, freq, cand_scores, freq_scores = carry
        here = lax.rem(me - step + owners, owners)
        one = lax.dot_general(
            hidden, cand, (((1,), (1,)), ((), ())), preferred_element_type=jnp.float32
        )
        panel = lax.dot_general(
            hidden, freq, (((1,), (1,)), ((), ())), preferred_element_type=jnp.float32
        )
        cand_scores = jnp.where((blocks == here)[:, :, None], one[:, None, :], cand_scores)
        freq_scores = jnp.where(
            (owner_order == here)[None, :, None], panel[:, None, :], freq_scores
        )
        return pass_on((cand, freq)) + (cand_scores, freq_scores)

    cand, freq, cand_scores, freq_scores = lax.fori_loop(
        0,
        owners,
        forward,
        (
            cand_embed,
            freq_embed,
            jnp.zeros((tokens, K, BW), jnp.float32),
            jnp.zeros((tokens, owners, PANEL), jnp.float32),
        ),
    )
    scores = jnp.concatenate(
        [freq_scores.reshape(tokens, freq_count), cand_scores.reshape(tokens, K * BW)], axis=1
    )
    top = jnp.max(scores, axis=1)
    exponentials = jnp.exp(scores - top[:, None])
    total = jnp.sum(exponentials, axis=1)
    columns = jnp.arange(scores.shape[1], dtype=jnp.int32)
    hot = (target_slot[:, None] == columns[None, :]).astype(jnp.float32)
    loss = jnp.log(total) + top - jnp.sum(hot * scores, axis=1)
    prob = (exponentials * (1.0 / total)[:, None] - hot).astype(jnp.bfloat16)
    prob_freq = prob[:, :freq_count].reshape(tokens, owners, PANEL)
    prob_cand = prob[:, freq_count:].reshape(tokens, K, BW)
    zero = jnp.zeros((), jnp.bfloat16)

    def backward(step, carry):
        cand, freq, grad_cand, grad_freq, grad_hidden = carry
        here = lax.rem(me - step + owners, owners)
        one = jnp.sum(jnp.where((blocks == here)[:, :, None], prob_cand, zero), axis=1)
        panel = jnp.sum(
            jnp.where((owner_order == here)[None, :, None], prob_freq, zero), axis=1
        )
        grad_hidden = (
            grad_hidden
            + jnp.dot(one, cand, preferred_element_type=jnp.float32)
            + jnp.dot(panel, freq, preferred_element_type=jnp.float32)
        )
        grad_cand = grad_cand + lax.dot_general(
            one, hidden, (((0,), (0,)), ((), ())), preferred_element_type=jnp.float32
        )
        grad_freq = grad_freq + lax.dot_general(
            panel, hidden, (((0,), (0,)), ((), ())), preferred_element_type=jnp.float32
        )
        return pass_on((cand, freq, grad_cand, grad_freq)) + (grad_hidden,)

    _, _, grad_cand, grad_freq, grad_hidden = lax.fori_loop(
        0,
        owners,
        backward,
        (
            cand,
            freq,
            jnp.zeros(cand.shape, jnp.float32),
            jnp.zeros(freq.shape, jnp.float32),
            jnp.zeros((tokens, D), jnp.float32),
        ),
    )

    def own_rows(whole):
        rows = whole.shape[0] // shards
        return lax.dynamic_slice_in_dim(lax.psum(whole, "token"), shard * rows, rows)

    return (
        scores.astype(jnp.bfloat16),
        loss,
        grad_hidden.astype(jnp.bfloat16),
        own_rows(grad_cand),
        own_rows(grad_freq),
    )


ROWS = BW + 16
HALF = D // 2
QUART = D // 4
ZDIM = 4
YDIM = 2
OWNERS = ZDIM * YDIM
SHARDS = 4
Y, UP, DOWN, X, CORE, CORE_X, HID, PROB, PROB_X, SUM_Y, SUM_UP, SUM_DOWN, FIN = range(13)
F32 = jnp.float32
BF16 = jnp.bfloat16
NT = (((1,), (1,)), ((), ()))
TN = (((0,), (0,)), ((), ()))


def kernel(
    hid, emb, freq, blk, tgt,
    logit_out, freq_out, loss_out, gh_out, gc_out, gf_out,
    table, hq, prob, scores, part, ysend, yrecv, zsend, zrecv, fin, finr,
    send, recv, local,
):
    v = lax.axis_index("vocab")
    t = lax.axis_index("token")
    z, y = v // YDIM, v % YDIM
    x, c = t // 2, t % 2
    ynb = (v + 1 - 2 * y, t)
    xs = (v, (1 - x) * 2 + c)
    cs = (v, x * 2 + 1 - c)
    dg = (v, (1 - x) * 2 + 1 - c)

    def along(step):
        return (v + step * YDIM, t)

    def both(distance, body):
        for sign in (-1, 1):
            zz = z + sign * distance
            ok = (zz >= 0) if sign < 0 else (zz < ZDIM)
            pl.when(ok)(lambda zz=zz, sign=sign: body(zz, sign))

    barrier = pltpu.get_barrier_semaphore()

    def greet(dev):
        pl.semaphore_signal(barrier, inc=1, device_id=dev, device_id_type=pl.DeviceIdType.MESH)

    loads = [
        pltpu.make_async_copy(emb, table.at[v, pl.ds(0, BW)], local.at[0]),
        pltpu.make_async_copy(freq, table.at[v, pl.ds(BW, 16)], local.at[1]),
    ]
    for one in loads:
        one.start()
    for dev in (ynb, xs, cs, dg):
        greet(dev)
    both(1, lambda zz, sign: greet(along(sign)))
    pl.semaphore_wait(barrier, 4 + (z + ZDIM - 1) // ZDIM + (2 * ZDIM - 2 - z) // ZDIM)
    for one in loads:
        one.wait()

    def copy(src, dst, kind, slot, dev):
        return pltpu.make_async_remote_copy(
            src_ref=src, dst_ref=dst, send_sem=send.at[kind, slot], recv_sem=recv.at[kind, slot],
            device_id=dev, device_id_type=pl.DeviceIdType.MESH,
        )

    def cols(start, width):
        return pl.ds(pl.multiple_of(start, QUART), width)

    my_half = cols(c * HALF, HALF)
    other_half = cols((1 - c) * HALF, HALF)

    def quarter(xx, cc):
        return cols((cc * 2 + xx) * QUART, QUART)

    my_q = quarter(x, c)
    xs_q = quarter(1 - x, c)

    def block(kind, vb, part_of, dev):
        view = table.at[vb, :, part_of]
        return copy(view, view, kind, vb, dev)

    def zkind(sign):
        return UP if sign > 0 else DOWN

    def hid_to(dev, xx, cc):
        return pltpu.make_async_remote_copy(
            src_ref=hid.at[:, quarter(xx, cc)], dst_ref=hq.at[t],
            send_sem=send.at[HID, dev[1]], recv_sem=recv.at[HID, t],
            device_id=dev, device_id_type=pl.DeviceIdType.MESH,
        )

    def hid_from(dev):
        return pltpu.make_async_remote_copy(
            src_ref=hid.at[:, my_q], dst_ref=hq.at[dev[1]],
            send_sem=send.at[HID, dev[1]], recv_sem=recv.at[HID, dev[1]],
            device_id=dev, device_id_type=pl.DeviceIdType.MESH,
        )

    both(1, lambda zz, sign: block(zkind(sign), v, my_half, along(sign)).start())
    block(Y, v, my_half, ynb).start()
    hid_to(xs, 1 - x, c).start()
    hid_to(dg, 1 - x, 1 - c).start()
    hid_to(cs, x, 1 - c).start()
    hq[t] = hid[:, my_q]

    def score(vb):
        def step(i, total):
            at = cols(i * QUART, QUART)
            return total + lax.dot_general(
                hid[:, at], table[vb, pl.ds(0, BW), at], NT, preferred_element_type=F32
            )

        scores[vb] = lax.fori_loop(0, 4, step, jnp.zeros((BW, BW), F32))

    score(v)

    def same_y(zz):
        return zz * YDIM + y

    def other_y(zz):
        return zz * YDIM + 1 - y

    def arrive_z(distance):
        def body(zz, sign):
            vb = same_y(zz)
            got = my_half if distance == 1 else my_q
            kind = zkind(-sign)
            block(kind, vb, got, ynb).wait_recv()
            onward = z - sign
            ok = (onward < ZDIM) if sign < 0 else (onward >= 0)
            pl.when(ok)(lambda: block(kind, vb, my_q, along(-sign)).start())
            block(Y, vb, my_q, ynb).start()
            if distance > 1:
                block(X, vb, my_q, xs).start()
            block(CORE, vb, got, cs).start()

        both(distance, body)

    def arrive_y(distance):
        def body(zz, sign):
            vb = other_y(zz)
            block(Y, vb, my_q, ynb).wait_recv()
            block(X, vb, my_q, xs).start()
            block(CORE, vb, my_q, cs).start()

        both(distance, body)

    def arrive_x(distance, of):
        def body(zz, sign):
            vb = of(zz)
            block(X, vb, xs_q, xs).wait_recv()
            block(CORE_X, vb, xs_q, cs).start()

        both(distance, body)

    def finish_half(vb):
        block(CORE, vb, other_half, cs).wait_recv()
        score(vb)

    def finish(distance, of):
        def body(zz, sign):
            vb = of(zz)
            block(CORE, vb, quarter(x, 1 - c), cs).wait_recv()
            block(CORE_X, vb, quarter(1 - x, 1 - c), cs).wait_recv()
            score(vb)

        both(distance, body)

    arrive_z(1)
    arrive_z(2)
    block(Y, other_y(z), my_half, ynb).wait_recv()
    block(CORE, other_y(z), my_half, cs).start()
    arrive_y(1)
    arrive_z(3)
    arrive_x(2, same_y)
    both(1, lambda zz, sign: finish_half(same_y(zz)))
    finish_half(other_y(z))
    arrive_x(1, other_y)
    arrive_y(2)
    finish(2, same_y)
    arrive_y(3)
    arrive_x(3, same_y)
    finish(1, other_y)
    arrive_x(2, other_y)
    arrive_x(3, other_y)
    finish(3, same_y)
    finish(2, other_y)
    finish(3, other_y)

    ftab = table[:, pl.ds(BW, 16), :].reshape(OWNERS * 16, D)
    fscores = lax.dot_general(hid[...], ftab, NT, preferred_element_type=F32)
    freq_out[...] = fscores
    lane = lax.broadcasted_iota(jnp.int32, (BW, BW), 1)
    flive = lane % 16 < PANEL
    low = F32(-3.0e38)

    def chosen(vb):
        return (
            (blk[:, 0:1] == vb) | (blk[:, 1:2] == vb) | (blk[:, 2:3] == vb) | (blk[:, 3:4] == vb)
        )

    high = jnp.where(flive, fscores, low)
    for vb in range(OWNERS):
        high = jnp.maximum(high, jnp.where(chosen(vb), scores[vb], low))
    top = jnp.max(high, axis=1, keepdims=True)
    fexp = jnp.where(flive, jnp.exp(jnp.where(flive, fscores, low) - top), 0.0)
    fhot = lane == tgt[:, 2:3]
    total = fexp
    picked = jnp.where(fhot, fscores, 0.0)
    for vb in range(OWNERS):
        total = total + jnp.where(chosen(vb), jnp.exp(jnp.where(chosen(vb), scores[vb], low) - top), 0.0)
        hot = (tgt[:, 0:1] == vb) & (lane == tgt[:, 1:2])
        picked = picked + jnp.where(hot, scores[vb], 0.0)
    total = jnp.sum(total, axis=1, keepdims=True)
    inverse = 1.0 / total
    for vb in range(OWNERS):
        live = chosen(vb)
        hot = ((tgt[:, 0:1] == vb) & (lane == tgt[:, 1:2])).astype(F32)
        value = jnp.where(live, jnp.exp(jnp.where(live, scores[vb], low) - top) * inverse, 0.0)
        prob[t, :, pl.ds(vb * BW, BW)] = (value - hot).astype(BF16)
    prob[t, :, pl.ds(OWNERS * BW, BW)] = (fexp * inverse - fhot.astype(F32)).astype(BF16)

    def prob_copy(kind, of, dev):
        return copy(prob.at[of], prob.at[of], kind, of, dev)

    prob_copy(PROB, t, xs).start()
    prob_copy(PROB_X, t, cs).start()

    loss = jnp.log(total) + top - jnp.sum(picked, axis=1, keepdims=True)
    loss_out[...] = jnp.broadcast_to(loss, (BW, BW))
    for k in range(K):
        mine = jnp.zeros((BW, BW), F32)
        for vb in range(OWNERS):
            mine = jnp.where(blk[:, k : k + 1] == vb, scores[vb], mine)
        logit_out[:, pl.ds(k * BW, BW)] = mine.astype(BF16)

    prob_copy(PROB, xs[1], xs).wait_recv()
    copy(prob.at[xs[1]], prob.at[xs[1]], PROB_X, xs[1], cs).start()
    hid_from(xs).wait_recv()
    hid_from(dg).wait_recv()
    hid_from(cs).wait_recv()
    prob_copy(PROB_X, cs[1], cs).wait_recv()
    prob_copy(PROB_X, dg[1], cs).wait_recv()

    tokens = SHARDS * BW
    fpart = lax.dot_general(
        prob[:, :, pl.ds(OWNERS * BW, BW)].reshape(tokens, BW),
        hq[...].reshape(tokens, QUART), TN, preferred_element_type=F32,
    ).reshape(ZDIM, YDIM, 16, QUART)
    fkeep = jnp.where(y == 0, fpart[:, 0], fpart[:, 1])
    fgive = jnp.where(y == 0, fpart[:, 1], fpart[:, 0])
    ysend[:, pl.ds(BW, 16), :] = fgive.astype(BF16)
    part[:, pl.ds(BW, 16), :] = fkeep

    def cand_part(vb):
        at = pl.ds(pl.multiple_of(vb * BW, BW), BW)
        return lax.dot_general(
            prob[:, :, at].reshape(tokens, BW), hq[...].reshape(tokens, QUART), TN,
            preferred_element_type=F32,
        )

    def sum_y(zz):
        return copy(ysend.at[zz], yrecv.at[zz], SUM_Y, zz, ynb)

    def give(zz, sign):
        ysend[zz, pl.ds(0, BW), :] = cand_part(other_y(zz)).astype(BF16)
        sum_y(zz).start()

    def keep(zz, sign):
        part[zz, pl.ds(0, BW), :] = cand_part(same_y(zz))

    for distance in (3, 2, 1):
        both(distance, give)
    give(z, 0)
    for distance in (3, 2, 1):
        both(distance, keep)
    keep(z, 0)

    def sum_z(zz, sign):
        kind = SUM_UP if sign > 0 else SUM_DOWN
        return copy(zsend.at[zz], zrecv.at[0 if sign > 0 else 1, zz], kind, zz, along(sign))

    def pass_on(zz, sign):
        sum_y(zz).wait_recv()
        behind = (z > 0) if sign > 0 else (z < ZDIM - 1)

        @pl.when(behind)
        def _():
            sum_z(zz, sign).wait_recv()
            zsend[zz] = (
                part[zz] + yrecv[zz].astype(F32) + zrecv[0 if sign > 0 else 1, zz].astype(F32)
            ).astype(BF16)

        @pl.when(jnp.logical_not(behind))
        def _():
            zsend[zz] = (part[zz] + yrecv[zz].astype(F32)).astype(BF16)

        sum_z(zz, sign).start()

    def grad_rows(i, carry):
        at = pl.ds(pl.multiple_of(i * 512, 512), 512)
        mine = prob[t]
        total = jnp.dot(
            mine[:, : OWNERS * BW], table[:, pl.ds(0, BW), at].reshape(OWNERS * BW, 512),
            preferred_element_type=F32,
        ) + jnp.dot(
            mine[:, OWNERS * BW :], table[:, pl.ds(BW, 16), at].reshape(OWNERS * 16, 512),
            preferred_element_type=F32,
        )
        gh_out[:, at] = total.astype(BF16)
        return carry

    both(3, pass_on)
    lax.fori_loop(0, 8, grad_rows, 0)
    both(2, pass_on)
    both(1, pass_on)
    sum_y(z).wait_recv()
    part[z] = part[z] + yrecv[z].astype(F32)

    def last(zz, sign):
        sum_z(z, -sign).wait_recv()
        part[z] = part[z] + zrecv[0 if sign < 0 else 1, z].astype(F32)

    both(1, last)
    for one in range(SHARDS):
        fin[one, pl.ds(0, 32), :] = part[z, pl.ds(one * 32, 32), :].astype(BF16)
        fin[one, pl.ds(32, 16), :] = part[z, pl.ds(BW, 16), :].astype(BF16)

    def fin_to(dev):
        return pltpu.make_async_remote_copy(
            src_ref=fin.at[dev[1]], dst_ref=finr.at[t],
            send_sem=send.at[FIN, dev[1]], recv_sem=recv.at[FIN, t],
            device_id=dev, device_id_type=pl.DeviceIdType.MESH,
        )

    def fin_from(dev):
        return pltpu.make_async_remote_copy(
            src_ref=fin.at[dev[1]], dst_ref=finr.at[dev[1]],
            send_sem=send.at[FIN, dev[1]], recv_sem=recv.at[FIN, dev[1]],
            device_id=dev, device_id_type=pl.DeviceIdType.MESH,
        )

    for dev in (xs, dg, cs):
        fin_to(dev).start()
    finr[t] = fin[t]

    both(1, lambda zz, sign: block(zkind(sign), v, my_half, along(sign)).wait_send())
    block(Y, v, my_half, ynb).wait_send()
    for dev in (xs, dg, cs):
        hid_to(dev, x, c).wait_send()
    block(CORE, other_y(z), my_half, cs).wait_send()
    for distance in (1, 2, 3):

        def sent(zz, sign, distance=distance):
            vb = same_y(zz)
            got = my_half if distance == 1 else my_q
            kind = zkind(-sign)
            onward = z - sign
            ok = (onward < ZDIM) if sign < 0 else (onward >= 0)
            pl.when(ok)(lambda: block(kind, vb, my_q, along(-sign)).wait_send())
            block(Y, vb, my_q, ynb).wait_send()
            block(CORE, vb, got, cs).wait_send()
            if distance > 1:
                block(X, vb, my_q, xs).wait_send()
                block(CORE_X, vb, xs_q, cs).wait_send()
            block(X, other_y(zz), my_q, xs).wait_send()
            block(CORE, other_y(zz), my_q, cs).wait_send()
            block(CORE_X, other_y(zz), xs_q, cs).wait_send()
            sum_y(zz).wait_send()
            sum_z(zz, sign).wait_send()

        both(distance, sent)
    sum_y(z).wait_send()
    prob_copy(PROB, t, xs).wait_send()
    prob_copy(PROB_X, t, cs).wait_send()
    prob_copy(PROB_X, xs[1], cs).wait_send()
    for dev in (xs, dg, cs):
        fin_to(dev).wait_send()
        fin_from(dev).wait_recv()

    row = lax.broadcasted_iota(jnp.int32, (16, QUART), 0)
    for one in range(SHARDS):
        place = (one % 2) * 2 + one // 2
        at = pl.ds(place * QUART, QUART)
        gc_out[:, at] = finr[one, pl.ds(0, 32), :].astype(F32)
        gf_out[:, at] = jnp.sum(
            jnp.where(row == t, finr[one, pl.ds(32, 16), :].astype(F32), 0.0), axis=0, keepdims=True
        )


def dense(hidden, cand_embed, freq_embed, owner_order, cand_blocks, group_tokens, target_slot):
    tokens = hidden.shape[0]
    freq_count = OWNERS * PANEL
    blocks = token_blocks(cand_blocks, group_tokens)
    in_cand = target_slot >= freq_count
    column = jnp.where(in_cand, target_slot - freq_count, 0)
    rank_hot = (column // BW)[:, None] == jnp.arange(K, dtype=jnp.int32)[None, :]
    target_block = jnp.where(in_cand, jnp.sum(jnp.where(rank_hot, blocks, 0), axis=1), -1)
    word = jnp.where(in_cand, column % BW, -1)
    slot = jnp.where(in_cand, 0, target_slot)
    panel_hot = (slot // PANEL)[:, None] == jnp.arange(OWNERS, dtype=jnp.int32)[None, :]
    panel = jnp.sum(jnp.where(panel_hot, owner_order[None, :], 0), axis=1)
    freq_lane = jnp.where(in_cand, -1, panel * 16 + slot % PANEL)
    tgt = jnp.stack([target_block, word, freq_lane, freq_lane], axis=1)
    freq_pad = jnp.pad(freq_embed, ((0, 16 - PANEL), (0, 0)))
    vmem = pl.BlockSpec(memory_space=pltpu.VMEM)
    hbm = pl.BlockSpec(memory_space=pl.ANY)
    shape = jax.ShapeDtypeStruct
    logits, freq_scores, loss, grad_hidden, grad_cand, grad_freq = pl.pallas_call(
        kernel,
        out_shape=(
            shape((tokens, K * BW), BF16),
            shape((tokens, BW), F32),
            shape((tokens, BW), F32),
            shape((tokens, D), BF16),
            shape((BW // SHARDS, D), F32),
            shape((1, D), F32),
        ),
        in_specs=[vmem, hbm, hbm, vmem, vmem],
        out_specs=(vmem,) * 6,
        scratch_shapes=[
            pltpu.VMEM((OWNERS, ROWS, D), BF16),
            pltpu.VMEM((SHARDS, BW, QUART), BF16),
            pltpu.VMEM((SHARDS, BW, OWNERS * BW + BW), BF16),
            pltpu.VMEM((OWNERS, BW, BW), F32),
            pltpu.VMEM((ZDIM, ROWS, QUART), F32),
            pltpu.VMEM((ZDIM, ROWS, QUART), BF16),
            pltpu.VMEM((ZDIM, ROWS, QUART), BF16),
            pltpu.VMEM((ZDIM, ROWS, QUART), BF16),
            pltpu.VMEM((2, ZDIM, ROWS, QUART), BF16),
            pltpu.VMEM((SHARDS, 48, QUART), BF16),
            pltpu.VMEM((SHARDS, 48, QUART), BF16),
            pltpu.SemaphoreType.DMA((13, OWNERS)),
            pltpu.SemaphoreType.DMA((13, OWNERS)),
            pltpu.SemaphoreType.DMA((2,)),
        ],
        compiler_params=pltpu.CompilerParams(
            collective_id=0, has_side_effects=True, vmem_limit_bytes=56 << 20
        ),
    )(hidden, cand_embed, freq_pad, blocks, tgt)
    panels = freq_scores.reshape(tokens, OWNERS, 16)[:, :, :PANEL]
    order_hot = owner_order[:, None] == jnp.arange(OWNERS, dtype=jnp.int32)[None, :]
    ordered = jnp.sum(
        jnp.where(order_hot[None, :, :, None], panels[:, None], 0.0), axis=2
    ).reshape(tokens, freq_count)
    all_logits = jnp.concatenate([ordered.astype(BF16), logits], axis=1)
    return (all_logits, loss[:, 0], grad_hidden, grad_cand, grad_freq)


def per_device(hidden, *rest):
    fits = (lax.axis_size("vocab"), lax.axis_size("token")) == (OWNERS, SHARDS)
    fits = fits and hidden.shape[0] == BW
    return (dense if fits else ring)(hidden, *rest)


def solution(mesh):
    in_specs = (
        P(("vocab", "token"), None),
        P("vocab", None),
        P("vocab", None),
        P(),
        P(("vocab", "token"), None),
        P(("vocab", "token"), None),
        P(("vocab", "token")),
    )
    out_specs = (
        P(("vocab", "token"), None),
        P(("vocab", "token")),
        P(("vocab", "token"), None),
        P(("vocab", "token"), None),
        P(("vocab", "token"), None),
    )
    return jax.shard_map(
        per_device, mesh=mesh, in_specs=in_specs, out_specs=out_specs, check_vma=False
    )
```
